32 devices in a mesh: row: 8 (over z, y), col: 4 (over x, core).
Axes of the slice: x: 2, y: 2, z: 4, core: 2. Of those that a mesh axis runs over, the one named last changes fastest.
Arguments:
- points: bfloat16 [64, 16384], P(None, ('row', 'col')), may hold values from -6 to 6
- lengths: float32 [64], replicated, may hold values from 0.5 to 2
- noise_var: float32 [16384], P(('row', 'col')), may hold values from 0.1 to 1
- solution: float32 [16, 16384], P(None, ('row', 'col')), may hold values from -6 to 6
- residual: float32 [16, 16384], P(None, ('row', 'col')), may hold values from -100 to 100
- direction: float32 [16, 16384], P(None, ('row', 'col')), may hold values from -100 to 100
Outputs:
- new_solution: float32 [16, 16384], P(None, ('row', 'col'))
- new_residual: float32 [16, 16384], P(None, ('row', 'col'))
- new_direction: float32 [16, 16384], P(None, ('row', 'col'))
The draws below stay inside these ranges and needn't reach their ends.
All inputs are finite; a program needn't handle non-finite values.
Results may differ from the reference program's by a relative error of at most 0.0043.
Values may be sent and summed in bfloat16 or wider, within the bound.
No kernel may reach another device: no remote copies, remote signals or barrier semaphores. Data moves between devices by JAX's collectives and lax.ppermute only.
A program may use at most 64 MiB of HBM per device.

```python
import math
import jax
import jax.numpy as jnp
from jax import lax

FEAT = 64
RHS = 16
POINTS = 16384


def scaled_field(key, top_scale):
    key_base = jax.random.fold_in(key, 0)
    key_rows = jax.random.fold_in(key, 2)
    key_cols = jax.random.fold_in(key, 3)
    base_draw = jax.random.truncated_normal(key_base, -4.0, 4.0, (RHS, POINTS), jnp.float32)
    mixed_draw = base_draw
    position = jnp.arange(POINTS, dtype=jnp.float32) / POINTS
    row_scale = jnp.exp(jax.random.uniform(key_rows, (POINTS,), jnp.float32, 0.0, math.log(top_scale)) + math.log(3.0) * position)
    col_scale = jnp.exp(jax.random.uniform(key_cols, (RHS, 1), jnp.float32, 0.0, math.log(10.0)))
    return mixed_draw * row_scale[None, :] * col_scale * 0.05


def draw_points(key, part):
    key = jax.random.fold_in(key, 11)
    key_latent, key_coef, key_jitter = jax.random.split(key, 3)
    span_size = 2.5
    latent = jax.random.uniform(key_latent, (4, POINTS), jnp.float32, -0.5, 0.5) * span_size
    coefficient = 0.25 * jax.random.uniform(key_coef, (FEAT,), jnp.float32, 0.6, 1.4)
    jitter = 0.1 * jax.random.truncated_normal(key_jitter, -4.0, 4.0, (FEAT, POINTS), jnp.float32)
    values = jnp.tile(latent, (FEAT // 4, 1)) * coefficient[:, None] + jitter
    return values.astype(jnp.bfloat16)


def draw_residual(key, part):
    key = jax.random.fold_in(key, 17)
    return scaled_field(key, 10.0)


def draw_direction(key, part):
    key = jax.random.fold_in(key, 23)
    return scaled_field(key, 10.0)


def steps_of(key, extent, cuts, least, top_value):
    level, own = 1.0, jax.random.fold_in(key, 6)
    for axis_at, parts in cuts:
        heights = jnp.exp(jax.random.uniform(jax.random.fold_in(own, axis_at), (parts,), jnp.float32, least / len(cuts), top_value / len(cuts)))
        level = level * jnp.repeat(heights, extent[axis_at] // parts).reshape([-1 if axis == axis_at else 1 for axis in range(len(extent))])
    return level


def scatter_about(own_key, extent, deviation, reach, cuts=(), kind=jnp.bfloat16):
    array = deviation * jax.random.normal(own_key, extent, jnp.float32)
    if cuts:
        array = array * steps_of(own_key, extent, cuts, -0.22, 0.18)
    return jnp.clip(array, -reach, reach).astype(kind)


def setup_inputs(seed: int = 0) -> dict:
    seeds = jax.random.split(jax.random.key(seed), 7)
    points = draw_points(jax.random.fold_in(seeds[6], 71), 0)
    lengths = jnp.clip(jnp.exp(jax.random.uniform(seeds[1], (FEAT,), jnp.float32, math.log(0.5), math.log(2.0))), 0.5, 2.0)
    noise_var = jnp.clip(jnp.exp(math.log(1.0) - 2.3025851 * jax.random.uniform(seeds[2], (POINTS,), jnp.float32) ** steps_of(seeds[2], (POINTS,), ((0, 32),), -0.2, 0.2)), 0.1, 1.0)
    solution = scatter_about(seeds[3], (RHS, POINTS), 1.0, 6.0, ((1, 32),), jnp.float32)
    residual = draw_residual(jax.random.fold_in(seeds[6], 71), 0)
    direction = draw_direction(jax.random.fold_in(seeds[6], 71), 0)
    return {"points": points, "lengths": lengths, "noise_var": noise_var, "solution": solution, "residual": residual, "direction": direction}


def reference(points, lengths, noise_var, solution, residual, direction):
    scaled = (points.astype(jnp.float32) / lengths[:, None]).astype(jnp.bfloat16)
    values = scaled.astype(jnp.float32)
    squares = jnp.sum(values * values, axis=0)
    narrow = direction.astype(jnp.bfloat16)
    block_rows = math.gcd(POINTS, 1024)

    def block_image(begin):
        part_scaled = lax.dynamic_slice_in_dim(scaled, begin, block_rows, 1)
        part_sq = lax.dynamic_slice_in_dim(squares, begin, block_rows, 0)
        cross_term = lax.dot_general(part_scaled, scaled, (((0,), (0,)), ((), ())), preferred_element_type=jnp.float32)
        kernel_tile = jnp.exp(-0.5 * (part_sq[:, None] + squares[None, :] - 2.0 * cross_term)).astype(jnp.bfloat16)
        return lax.dot_general(narrow, kernel_tile, (((1,), (1,)), ((), ())), preferred_element_type=jnp.float32)

    starts = jnp.arange(POINTS // block_rows, dtype=jnp.int32) * block_rows
    pieces = lax.map(block_image, starts)
    kernel_part = jnp.transpose(pieces, (1, 0, 2)).reshape(RHS, POINTS)
    image_field = kernel_part + noise_var[None, :] * direction
    norm_old = jnp.sum(residual * residual, axis=1)
    curvature = jnp.sum(direction * image_field, axis=1)
    step_size = norm_old / curvature
    new_solution = solution + step_size[:, None] * direction
    new_residual = residual - step_size[:, None] * image_field
    norm_new = jnp.sum(new_residual * new_residual, axis=1)
    new_direction = new_residual + (norm_new / norm_old)[:, None] * direction
    return (new_solution, new_residual, new_direction)
```

```python
import functools

import jax
import jax.numpy as jnp
from jax import lax
from jax.experimental import pallas as pl
from jax.experimental.pallas import tpu as pltpu
from jax.sharding import PartitionSpec as P

AXES = ("row", "col")
X, Y = 2, 4
CORE = 1
LINE = 8
LOG2E = 1.4426950408889634
TAIL = 16
UNROLL = 16
VMEM_LIMIT = 24 * 1024 * 1024


def params():
    return pltpu.CompilerParams(vmem_limit_bytes=VMEM_LIMIT)


def three_pieces(value):
    high = value.astype(jnp.bfloat16).astype(jnp.float32)
    rest = value - high
    middle = rest.astype(jnp.bfloat16).astype(jnp.float32)
    return high, middle, rest - middle


def tail_rows(squares, first):
    count = squares.shape[1]
    high, middle, low = three_pieces(-0.5 * squares)
    at = lax.broadcasted_iota(jnp.int32, (TAIL, count), 0)
    start = 0 if first else 3
    tail = jnp.where(at < 6, 1.0, 0.0)
    tail = jnp.where(at == start, high, tail)
    tail = jnp.where(at == start + 1, middle, tail)
    tail = jnp.where(at == start + 2, low, tail)
    return tail


def scaled_of(points, lengths):
    return (points.astype(jnp.float32) / lengths).astype(jnp.bfloat16)


def squares_of(scaled):
    values = scaled.astype(jnp.float32)
    return jnp.sum(values * values, axis=0, keepdims=True)


def side_of(points, lengths, first):
    scaled = scaled_of(points, lengths)
    tail = tail_rows(squares_of(scaled), first)
    return jnp.concatenate([scaled.astype(jnp.float32), tail], axis=0)


def put_row_side(ref, points, lengths):
    ref[...] = side_of(points, lengths, True).T.astype(jnp.bfloat16)


def put_col_side(ref, points, lengths):
    ref[...] = side_of(points, lengths, False).astype(jnp.bfloat16)


def half_distance(row_ref, col_ref):
    return jnp.dot(row_ref[...], col_ref[...], preferred_element_type=jnp.float32)


def add_product(out_ref, half, weight_ref):
    tile = jnp.exp2(half * LOG2E).astype(jnp.bfloat16)
    out_ref[...] += lax.dot_general(
        weight_ref[...], tile, (((1,), (1,)), ((), ())), preferred_element_type=jnp.float32
    )


def add_all(out_refs, row_refs, segments, held):
    rows = len(out_refs)

    def tiles(sides, blocks, feat, begin, count):
        return [
            (out_refs[row], row_refs[row], sides.at[begin + at], blocks.at[begin + at, feat:])
            for at in range(count)
            for row in range(rows)
        ]

    def run(order, half, last):
        for place, (out_ref, _, _, weight_ref) in enumerate(order):
            if place + 1 < len(order):
                ahead = half_distance(*order[place + 1][1:3])
            else:
                ahead = last()
            add_product(out_ref, half, weight_ref)
            half = ahead

    if sum(segment[0].shape[0] for segment in segments) * rows <= UNROLL:
        order = [tile for segment in segments for tile in tiles(*segment, 0, segment[0].shape[0])]
        run(order, half_distance(*order[0][1:3]), lambda: None)
        return

    for sides, blocks, feat in segments:
        cols = sides.shape[0]
        group = max(at for at in range(1, cols + 1) if cols % at == 0 and at * rows <= max(UNROLL, rows))

        def following(begin):
            held[...] = half_distance(row_refs[0], sides.at[begin])

        def body(index, _):
            order = tiles(sides, blocks, feat, index * group, group)
            run(order, held[...], lambda: following((index + 1) * group))
            return 0

        following(0)
        steps = cols // group
        lax.fori_loop(0, steps - 1, body, 0)
        run(tiles(sides, blocks, feat, (steps - 1) * group, group), held[...], lambda: None)


def pack_kernel(points_ref, direction_ref, out_ref, points_out_ref, wide, sems):
    feat = points_ref.shape[0]
    copies = (
        pltpu.make_async_copy(direction_ref, wide, sems.at[0]),
        pltpu.make_async_copy(points_ref, out_ref.at[:feat], sems.at[1]),
    )
    for copy in copies:
        copy.start()
    copies[0].wait()
    out_ref[feat:] = wide[...].astype(jnp.bfloat16)
    copies[1].wait()
    points_out_ref[...] = out_ref[:feat]


def pair_kernel(own_ref, other_ref, pair_ref):
    pair_ref[0] = own_ref[...]
    pair_ref[1] = other_ref[...]


def put_col_sides(col_side, blocks_ref, feat, lengths):
    for at in range(col_side.shape[0]):
        put_col_side(col_side.at[at], blocks_ref[at, :feat], lengths)


def chip_kernel(peers, feat, lengths_ref, pair_ref, *refs):
    points_refs, out_refs = refs[:peers], refs[peers : 2 * peers + 1]
    row_side, col_side, held = refs[2 * peers + 1 :]
    lengths = lengths_ref[...]
    put_col_sides(col_side, pair_ref, feat, lengths)
    for at, ref in enumerate((pair_ref.at[0, :feat], *points_refs)):
        put_row_side(row_side.at[at], ref[...], lengths)
        out_refs[at][...] = jnp.zeros_like(out_refs[at])
    add_all(
        out_refs,
        [row_side.at[at] for at in range(peers + 1)],
        [(col_side, pair_ref, feat)],
        held,
    )


def across_kernel(feat, lengths_ref, pair_ref, pair_side, points_ref, out_ref, row_side, held):
    put_row_side(row_side, points_ref[...], lengths_ref[...])
    out_ref[...] = jnp.zeros_like(out_ref)
    add_all([out_ref], [row_side], [(pair_side, pair_ref, feat)], held)


def onward_kernel(_, *refs):
    for at, ref in enumerate(refs[:-1]):
        refs[-1][at] = ref[...]


def peers_kernel(feat, lengths_ref, blocks_ref, across_side, near_sides, *refs):
    col_side, held = refs[-2:]
    peers = near_sides.shape[0]
    start_refs, out_refs = refs[:peers], refs[peers:-2]
    put_col_sides(col_side, blocks_ref, feat, lengths_ref[...])
    for start_ref, out_ref in zip(start_refs, out_refs):
        out_ref[...] = start_ref[...]
    add_all(
        out_refs,
        [across_side] + [near_sides.at[at] for at in range(1, peers)],
        [(col_side, blocks_ref, feat)],
        held,
    )


def last_kernel(feat, sides_ref, start_ref, line_ref, line_side, blocks_ref, blocks_side, out_ref, held):
    out_ref[...] = start_ref[...]
    add_all(
        [out_ref], [sides_ref.at[0]], [(line_side, line_ref, feat), (blocks_side, blocks_ref, feat)], held
    )


def cost(pairs):
    return pl.CostEstimate(flops=pairs * 768, bytes_accessed=pairs // 4, transcendentals=pairs)


def scattered_kernel(parts, *refs):
    noise_ref, direction_ref, residual_ref = refs[:3]
    image_ref, sums_ref = refs[3 + parts :]
    direction, residual = direction_ref[...], residual_ref[...]
    image = noise_ref[...] * direction
    for ref in refs[3 : 3 + parts]:
        image = image + ref[...]
    image_ref[...] = image
    sums = (
        jnp.sum(residual * residual, axis=1, keepdims=True),
        jnp.sum(direction * image, axis=1, keepdims=True),
        jnp.sum(residual * image, axis=1, keepdims=True),
        jnp.sum(image * image, axis=1, keepdims=True),
    )
    rhs = direction.shape[0]
    lane = lax.broadcasted_iota(jnp.int32, (rhs, 128), 1)
    right = lax.broadcasted_iota(jnp.int32, (rhs, 128), 0)
    packed = jnp.zeros((rhs, 128), jnp.float32)
    for index, value in enumerate(sums):
        packed = jnp.where(lane == index * rhs + right, value, packed)
    row = jnp.sum(packed, axis=0, keepdims=True)
    sums_ref[...] = jnp.broadcast_to(row[None], sums_ref.shape)


def update_kernel(
    solution_ref, residual_ref, direction_ref, image_ref, sums_ref, new_solution, new_residual, new_direction
):
    direction = direction_ref[...]
    rhs = direction.shape[0]
    row = jnp.sum(sums_ref[...], axis=0)
    lane = lax.broadcasted_iota(jnp.int32, (rhs, 128), 1)
    right = lax.broadcasted_iota(jnp.int32, (rhs, 128), 0)
    norm_old, curvature, mixed, image_norm = (
        jnp.sum(jnp.where(lane == index * rhs + right, row, 0.0), axis=1, keepdims=True)
        for index in range(4)
    )
    step = norm_old / curvature
    norm_new = jnp.maximum(norm_old + step * (step * image_norm - 2.0 * mixed), 0.0)
    updated = residual_ref[...] - step * image_ref[...]
    new_solution[...] = solution_ref[...] + step * direction
    new_residual[...] = updated
    new_direction[...] = updated + (norm_new / norm_old) * direction


def swap(array, devices, mask):
    return lax.ppermute(array, AXES, [(at, at ^ mask) for at in range(devices)])


def local(devices, points, lengths, noise_var, solution, residual, direction):
    f32, bf16 = jnp.float32, jnp.bfloat16
    shape = jax.ShapeDtypeStruct
    feat, width = points.shape
    rhs = direction.shape[0]
    depth = feat + TAIL
    masks = (X + Y, X, Y)
    peers = len(masks)
    line_count = devices // LINE - 1
    tile_pairs = width * width
    held = pltpu.VMEM((width, width), f32)
    partial_shape = shape((rhs, width), f32)
    lengths = lengths[:, None]

    along_x = swap(points, devices, X)
    packed, near = pl.pallas_call(
        pack_kernel,
        out_shape=[shape((feat + rhs, width), bf16), shape((feat, width), bf16)],
        in_specs=[pl.BlockSpec(memory_space=pltpu.HBM)] * 2,
        scratch_shapes=[pltpu.VMEM((rhs, width), f32), pltpu.SemaphoreType.DMA((2,))],
        compiler_params=params(),
    )(
        pltpu.with_memory_space_constraint(points, pltpu.HBM),
        pltpu.with_memory_space_constraint(direction, pltpu.HBM),
    )
    line = [swap(packed, devices, LINE * at) for at in range(1, line_count + 1)]
    along_y = swap(near, devices, Y)
    across = swap(along_x, devices, Y)
    pair = pl.pallas_call(
        pair_kernel, out_shape=shape((2, feat + rhs, width), bf16), compiler_params=params()
    )(packed, swap(packed, devices, CORE))

    own, x_partial, y_partial, near_sides, pair_side = pl.pallas_call(
        functools.partial(chip_kernel, 2, feat),
        out_shape=[partial_shape] * 3
        + [shape((3, width, depth), bf16), shape((2, depth, width), bf16)],
        scratch_shapes=[held],
        compiler_params=params(),
        cost_estimate=cost(tile_pairs // 2),
    )(lengths, pair, along_x, along_y)
    across_partial, across_side = pl.pallas_call(
        functools.partial(across_kernel, feat),
        out_shape=[partial_shape, shape((width, depth), bf16)],
        scratch_shapes=[held],
        compiler_params=params(),
        cost_estimate=cost(tile_pairs // 2),
    )(lengths, pair, pair_side, across)
    for_peers = [across_partial, x_partial, y_partial]
    onward = pl.pallas_call(
        onward_kernel,
        out_shape=shape((line_count, feat + rhs, width), bf16),
        in_specs=[pl.BlockSpec(memory_space=pl.ANY)]
        + [pl.BlockSpec(memory_space=pltpu.VMEM)] * line_count,
        compiler_params=params(),
    )(for_peers[0], *line)
    blocks = swap(onward, devices, CORE)
    sides = []
    for columns in (onward, blocks):
        *for_peers, side = pl.pallas_call(
            functools.partial(peers_kernel, feat),
            out_shape=[partial_shape] * peers + [shape((line_count, depth, width), bf16)],
            scratch_shapes=[held],
            compiler_params=params(),
            cost_estimate=cost(peers * line_count * tile_pairs),
        )(lengths, columns, across_side, near_sides, *for_peers)
        sides.append(side)
    from_peers = [swap(part, devices, mask) for part, mask in zip(for_peers, masks)]
    mine = pl.pallas_call(
        functools.partial(last_kernel, feat),
        out_shape=partial_shape,
        scratch_shapes=[held],
        compiler_params=params(),
        cost_estimate=cost(2 * line_count * tile_pairs),
    )(near_sides, own, onward, sides[0], blocks, sides[1])

    image, sums = pl.pallas_call(
        functools.partial(scattered_kernel, 1 + peers),
        out_shape=[shape((rhs, width), f32), shape((devices, 1, 128), f32)],
        compiler_params=params(),
    )(noise_var[None, :], direction, residual, mine, *from_peers)
    all_sums = lax.all_to_all(sums, AXES, 0, 0, tiled=True)
    return tuple(
        pl.pallas_call(
            update_kernel, out_shape=[shape((rhs, width), f32)] * 3, compiler_params=params()
        )(solution, residual, direction, image, all_sums)
    )


def solution(mesh):
    placed = (
        P(None, AXES),
        P(),
        P(AXES),
        P(None, AXES),
        P(None, AXES),
        P(None, AXES),
    )
    return jax.shard_map(
        functools.partial(local, mesh.shape["row"] * mesh.shape["col"]),
        mesh=mesh,
        in_specs=placed,
        out_specs=(P(None, AXES), P(None, AXES), P(None, AXES)),
        check_vma=False,
    )
```

```python
import functools

import jax
import jax.numpy as jnp
from jax import lax
from jax.experimental import pallas as pl
from jax.experimental.pallas import tpu as pltpu
from jax.sharding import PartitionSpec as P

AXES = ("row", "col")
X, Y = 2, 4
CORE = 1
LINE = 8
LOG2E = 1.4426950408889634
TAIL = 16
UNROLL = 16
VMEM_LIMIT = 24 * 1024 * 1024


def params():
    return pltpu.CompilerParams(vmem_limit_bytes=VMEM_LIMIT)


def three_pieces(value):
    high = value.astype(jnp.bfloat16).astype(jnp.float32)
    rest = value - high
    middle = rest.astype(jnp.bfloat16).astype(jnp.float32)
    return high, middle, rest - middle


def tail_rows(squares, first):
    count = squares.shape[1]
    high, middle, low = three_pieces(-0.5 * squares)
    at = lax.broadcasted_iota(jnp.int32, (TAIL, count), 0)
    start = 0 if first else 3
    tail = jnp.where(at < 6, 1.0, 0.0)
    tail = jnp.where(at == start, high, tail)
    tail = jnp.where(at == start + 1, middle, tail)
    tail = jnp.where(at == start + 2, low, tail)
    return tail


def scaled_of(points, lengths):
    return (points.astype(jnp.float32) / lengths).astype(jnp.bfloat16)


def squares_of(scaled):
    values = scaled.astype(jnp.float32)
    return jnp.sum(values * values, axis=0, keepdims=True)


def side_of(points, lengths, first):
    scaled = scaled_of(points, lengths)
    tail = tail_rows(squares_of(scaled), first)
    return jnp.concatenate([scaled.astype(jnp.float32), tail], axis=0)


def put_row_side(ref, points, lengths):
    ref[...] = side_of(points, lengths, True).T.astype(jnp.bfloat16)


def put_col_side(ref, points, lengths):
    ref[...] = side_of(points, lengths, False).astype(jnp.bfloat16)


def half_distance(row_ref, col_ref):
    return jnp.dot(row_ref[...], col_ref[...], preferred_element_type=jnp.float32)


def add_product(out_ref, half, weight_ref):
    tile = jnp.exp2(half * LOG2E).astype(jnp.bfloat16)
    out_ref[...] += lax.dot_general(
        weight_ref[...], tile, (((1,), (1,)), ((), ())), preferred_element_type=jnp.float32
    )


def add_all(out_refs, row_refs, segments, held):
    rows = len(out_refs)

    def tiles(sides, blocks, feat, begin, count):
        return [
            (out_refs[row], row_refs[row], sides.at[begin + at], blocks.at[begin + at, feat:])
            for at in range(count)
            for row in range(rows)
        ]

    def run(order, half, last):
        for place, (out_ref, _, _, weight_ref) in enumerate(order):
            if place + 1 < len(order):
                ahead = half_distance(*order[place + 1][1:3])
            else:
                ahead = last()
            add_product(out_ref, half, weight_ref)
            half = ahead

    if sum(segment[0].shape[0] for segment in segments) * rows <= UNROLL:
        order = [tile for segment in segments for tile in tiles(*segment, 0, segment[0].shape[0])]
        run(order, half_distance(*order[0][1:3]), lambda: None)
        return

    for sides, blocks, feat in segments:
        cols = sides.shape[0]
        group = max(at for at in range(1, cols + 1) if cols % at == 0 and at * rows <= max(UNROLL, rows))

        def following(begin):
            held[...] = half_distance(row_refs[0], sides.at[begin])

        def body(index, _):
            order = tiles(sides, blocks, feat, index * group, group)
            run(order, held[...], lambda: following((index + 1) * group))
            return 0

        following(0)
        steps = cols // group
        lax.fori_loop(0, steps - 1, body, 0)
        run(tiles(sides, blocks, feat, (steps - 1) * group, group), held[...], lambda: None)


def pack_kernel(points_ref, direction_ref, out_ref, points_out_ref, wide, sems):
    feat = points_ref.shape[0]
    copies = (
        pltpu.make_async_copy(direction_ref, wide, sems.at[0]),
        pltpu.make_async_copy(points_ref, out_ref.at[:feat], sems.at[1]),
    )
    for copy in copies:
        copy.start()
    copies[0].wait()
    out_ref[feat:] = wide[...].astype(jnp.bfloat16)
    copies[1].wait()
    points_out_ref[...] = out_ref[:feat]


def pair_kernel(own_ref, other_ref, pair_ref):
    pair_ref[0] = own_ref[...]
    pair_ref[1] = other_ref[...]


def put_col_sides(col_side, blocks_ref, feat, lengths):
    for at in range(col_side.shape[0]):
        put_col_side(col_side.at[at], blocks_ref[at, :feat], lengths)


def chip_kernel(peers, feat, lengths_ref, pair_ref, *refs):
    points_refs, out_refs = refs[:peers], refs[peers : 2 * peers + 1]
    row_side, col_side, held = refs[2 * peers + 1 :]
    lengths = lengths_ref[...]
    put_col_sides(col_side, pair_ref, feat, lengths)
    for at, ref in enumerate((pair_ref.at[0, :feat], *points_refs)):
        put_row_side(row_side.at[at], ref[...], lengths)
        out_refs[at][...] = jnp.zeros_like(out_refs[at])
    add_all(
        out_refs,
        [row_side.at[at] for at in range(peers + 1)],
        [(col_side, pair_ref, feat)],
        held,
    )


def across_kernel(feat, lengths_ref, pair_ref, pair_side, points_ref, out_ref, row_side, held):
    put_row_side(row_side, points_ref[...], lengths_ref[...])
    out_ref[...] = jnp.zeros_like(out_ref)
    add_all([out_ref], [row_side], [(pair_side, pair_ref, feat)], held)


def onward_kernel(_, *refs):
    for at, ref in enumerate(refs[:-1]):
        refs[-1][at] = ref[...]


def peers_kernel(feat, lengths_ref, blocks_ref, across_side, near_sides, *refs):
    col_side, held = refs[-2:]
    peers = near_sides.shape[0]
    start_refs, out_refs = refs[:peers], refs[peers:-2]
    put_col_sides(col_side, blocks_ref, feat, lengths_ref[...])
    for start_ref, out_ref in zip(start_refs, out_refs):
        out_ref[...] = start_ref[...]
    add_all(
        out_refs,
        [across_side] + [near_sides.at[at] for at in range(1, peers)],
        [(col_side, blocks_ref, feat)],
        held,
    )


def last_kernel(feat, sides_ref, start_ref, line_ref, line_side, blocks_ref, blocks_side, out_ref, held):
    out_ref[...] = start_ref[...]
    add_all(
        [out_ref], [sides_ref.at[0]], [(line_side, line_ref, feat), (blocks_side, blocks_ref, feat)], held
    )


def cost(pairs):
    return pl.CostEstimate(flops=pairs * 768, bytes_accessed=pairs // 4, transcendentals=pairs)


def scattered_kernel(parts, *refs):
    noise_ref, direction_ref, residual_ref = refs[:3]
    image_ref, sums_ref = refs[3 + parts :]
    direction, residual = direction_ref[...], residual_ref[...]
    image = noise_ref[...] * direction
    for ref in refs[3 : 3 + parts]:
        image = image + ref[...]
    image_ref[...] = image
    sums = (
        jnp.sum(residual * residual, axis=1, keepdims=True),
        jnp.sum(direction * image, axis=1, keepdims=True),
        jnp.sum(residual * image, axis=1, keepdims=True),
        jnp.sum(image * image, axis=1, keepdims=True),
    )
    rhs = direction.shape[0]
    lane = lax.broadcasted_iota(jnp.int32, (rhs, 128), 1)
    right = lax.broadcasted_iota(jnp.int32, (rhs, 128), 0)
    packed = jnp.zeros((rhs, 128), jnp.float32)
    for index, value in enumerate(sums):
        packed = jnp.where(lane == index * rhs + right, value, packed)
    row = jnp.sum(packed, axis=0, keepdims=True)
    sums_ref[...] = jnp.broadcast_to(row[None], sums_ref.shape)


def update_kernel(
    solution_ref, residual_ref, direction_ref, image_ref, sums_ref, new_solution, new_residual, new_direction
):
    direction = direction_ref[...]
    rhs = direction.shape[0]
    row = jnp.sum(sums_ref[...], axis=0)
    lane = lax.broadcasted_iota(jnp.int32, (rhs, 128), 1)
    right = lax.broadcasted_iota(jnp.int32, (rhs, 128), 0)
    norm_old, curvature, mixed, image_norm = (
        jnp.sum(jnp.where(lane == index * rhs + right, row, 0.0), axis=1, keepdims=True)
        for index in range(4)
    )
    step = norm_old / curvature
    norm_new = jnp.maximum(norm_old + step * (step * image_norm - 2.0 * mixed), 0.0)
    updated = residual_ref[...] - step * image_ref[...]
    new_solution[...] = solution_ref[...] + step * direction
    new_residual[...] = updated
    new_direction[...] = updated + (norm_new / norm_old) * direction


def swap(array, devices, mask):
    return lax.ppermute(array, AXES, [(at, at ^ mask) for at in range(devices)])


def shift_line(array, devices, steps):
    return lax.ppermute(
        array, AXES, [(at, (at + steps * LINE) % devices) for at in range(devices)]
    )


def local(devices, points, lengths, noise_var, solution, residual, direction):
    f32, bf16 = jnp.float32, jnp.bfloat16
    shape = jax.ShapeDtypeStruct
    feat, width = points.shape
    rhs = direction.shape[0]
    depth = feat + TAIL
    masks = (X + Y, X, Y)
    peers = len(masks)
    line_count = devices // LINE - 1
    tile_pairs = width * width
    held = pltpu.VMEM((width, width), f32)
    partial_shape = shape((rhs, width), f32)
    lengths = lengths[:, None]

    along_x = swap(points, devices, X)
    packed, near = pl.pallas_call(
        pack_kernel,
        out_shape=[shape((feat + rhs, width), bf16), shape((feat, width), bf16)],
        in_specs=[pl.BlockSpec(memory_space=pltpu.HBM)] * 2,
        scratch_shapes=[pltpu.VMEM((rhs, width), f32), pltpu.SemaphoreType.DMA((2,))],
        compiler_params=params(),
    )(
        pltpu.with_memory_space_constraint(points, pltpu.HBM),
        pltpu.with_memory_space_constraint(direction, pltpu.HBM),
    )
    line = [shift_line(packed, devices, steps) for steps in range(line_count, 0, -1)]
    along_y = swap(near, devices, Y)
    across = swap(along_x, devices, Y)
    pair = pl.pallas_call(
        pair_kernel, out_shape=shape((2, feat + rhs, width), bf16), compiler_params=params()
    )(packed, swap(packed, devices, CORE))

    own, x_partial, y_partial, near_sides, pair_side = pl.pallas_call(
        functools.partial(chip_kernel, 2, feat),
        out_shape=[partial_shape] * 3
        + [shape((3, width, depth), bf16), shape((2, depth, width), bf16)],
        scratch_shapes=[held],
        compiler_params=params(),
        cost_estimate=cost(tile_pairs // 2),
    )(lengths, pair, along_x, along_y)
    across_partial, across_side = pl.pallas_call(
        functools.partial(across_kernel, feat),
        out_shape=[partial_shape, shape((width, depth), bf16)],
        scratch_shapes=[held],
        compiler_params=params(),
        cost_estimate=cost(tile_pairs // 2),
    )(lengths, pair, pair_side, across)
    for_peers = [across_partial, x_partial, y_partial]
    onward = pl.pallas_call(
        onward_kernel,
        out_shape=shape((line_count, feat + rhs, width), bf16),
        in_specs=[pl.BlockSpec(memory_space=pl.ANY)]
        + [pl.BlockSpec(memory_space=pltpu.VMEM)] * line_count,
        compiler_params=params(),
    )(for_peers[0], *line)
    blocks = swap(onward, devices, CORE)
    sides = []
    for columns in (onward, blocks):
        *for_peers, side = pl.pallas_call(
            functools.partial(peers_kernel, feat),
            out_shape=[partial_shape] * peers + [shape((line_count, depth, width), bf16)],
            scratch_shapes=[held],
            compiler_params=params(),
            cost_estimate=cost(peers * line_count * tile_pairs),
        )(lengths, columns, across_side, near_sides, *for_peers)
        sides.append(side)
    from_peers = [swap(part, devices, mask) for part, mask in zip(for_peers, masks)]
    mine = pl.pallas_call(
        functools.partial(last_kernel, feat),
        out_shape=partial_shape,
        scratch_shapes=[held],
        compiler_params=params(),
        cost_estimate=cost(2 * line_count * tile_pairs),
    )(near_sides, own, onward, sides[0], blocks, sides[1])

    image, sums = pl.pallas_call(
        functools.partial(scattered_kernel, 1 + peers),
        out_shape=[shape((rhs, width), f32), shape((devices, 1, 128), f32)],
        compiler_params=params(),
    )(noise_var[None, :], direction, residual, mine, *from_peers)
    all_sums = lax.all_to_all(sums, AXES, 0, 0, tiled=True)
    return tuple(
        pl.pallas_call(
            update_kernel, out_shape=[shape((rhs, width), f32)] * 3, compiler_params=params()
        )(solution, residual, direction, image, all_sums)
    )


def solution(mesh):
    placed = (
        P(None, AXES),
        P(),
        P(AXES),
        P(None, AXES),
        P(None, AXES),
        P(None, AXES),
    )
    return jax.shard_map(
        functools.partial(local, mesh.shape["row"] * mesh.shape["col"]),
        mesh=mesh,
        in_specs=placed,
        out_specs=(P(None, AXES), P(None, AXES), P(None, AXES)),
        check_vma=False,
    )
```

```python
import functools
from typing import Any, NamedTuple

import jax
import jax.numpy as jnp
from jax import lax
from jax.experimental import pallas as pl
from jax.experimental.pallas import tpu as pltpu
from jax.sharding import PartitionSpec as P

AXES = ("row", "col")
X, Y = 2, 4
CORE = 1
LINE = 8
LOG2E = 1.4426950408889634
TAIL = 16
UNROLL = 16
EARLY, LATE = 0.25, 6
VMEM_LIMIT = 24 * 1024 * 1024


def params():
    return pltpu.CompilerParams(vmem_limit_bytes=VMEM_LIMIT)


def three_pieces(value):
    high = value.astype(jnp.bfloat16).astype(jnp.float32)
    rest = value - high
    middle = rest.astype(jnp.bfloat16).astype(jnp.float32)
    return high, middle, rest - middle


def tail_rows(squares, first):
    count = squares.shape[1]
    high, middle, low = three_pieces(-0.5 * squares)
    at = lax.broadcasted_iota(jnp.int32, (TAIL, count), 0)
    start = 0 if first else 3
    tail = jnp.where(at < 6, 1.0, 0.0)
    tail = jnp.where(at == start, high, tail)
    tail = jnp.where(at == start + 1, middle, tail)
    tail = jnp.where(at == start + 2, low, tail)
    return tail


def scaled_of(points, lengths):
    return (points.astype(jnp.float32) / lengths).astype(jnp.bfloat16)


def squares_of(scaled):
    values = scaled.astype(jnp.float32)
    return jnp.sum(values * values, axis=0, keepdims=True)


def side_of(points, lengths, first):
    scaled = scaled_of(points, lengths)
    tail = tail_rows(squares_of(scaled), first)
    return jnp.concatenate([scaled.astype(jnp.float32), tail], axis=0)


def put_row_side(ref, points, lengths):
    ref[...] = side_of(points, lengths, True).T.astype(jnp.bfloat16)


def put_col_side(ref, points, lengths):
    ref[...] = side_of(points, lengths, False).astype(jnp.bfloat16)


def half_distance(row_ref, col_ref):
    return jnp.dot(row_ref[...], col_ref[...], preferred_element_type=jnp.float32)


def add_product(out_ref, half, weight_ref):
    tile = jnp.exp2(half * LOG2E).astype(jnp.bfloat16)
    out_ref[...] += lax.dot_general(
        weight_ref[...], tile, (((1,), (1,)), ((), ())), preferred_element_type=jnp.float32
    )


def add_all(groups, feat, held):
    def tiles(rows, sides, blocks, begin, count):
        return [
            (out_ref, row_ref, sides.at[begin + at], blocks.at[begin + at, feat:])
            for at in range(count)
            for out_ref, row_ref in rows
        ]

    def run(order, half, last):
        for place, (out_ref, _, _, weight_ref) in enumerate(order):
            if place + 1 < len(order):
                ahead = half_distance(*order[place + 1][1:3])
            else:
                ahead = last()
            add_product(out_ref, half, weight_ref)
            half = ahead

    pieces = [(rows, sides, blocks) for rows, cols in groups for sides, blocks in cols]
    if sum(len(rows) * sides.shape[0] for rows, sides, _ in pieces) <= UNROLL:
        order = [tile for piece in pieces for tile in tiles(*piece, 0, piece[1].shape[0])]
        run(order, half_distance(*order[0][1:3]), lambda: None)
        return

    for rows, sides, blocks in pieces:
        cols = sides.shape[0]
        group = max(
            at for at in range(1, cols + 1) if cols % at == 0 and (at == 1 or at * len(rows) <= UNROLL)
        )

        def following(begin):
            held[...] = half_distance(rows[0][1], sides.at[begin])

        def body(index, _):
            order = tiles(rows, sides, blocks, index * group, group)
            run(order, held[...], lambda: following((index + 1) * group))
            return 0

        following(0)
        steps = cols // group
        lax.fori_loop(0, steps - 1, body, 0)
        run(tiles(rows, sides, blocks, (steps - 1) * group, group), held[...], lambda: None)


def pack_kernel(points_ref, direction_ref, out_ref, wide, sems):
    feat = points_ref.shape[0]
    copies = (
        pltpu.make_async_copy(direction_ref, wide, sems.at[0]),
        pltpu.make_async_copy(points_ref, out_ref.at[:feat], sems.at[1]),
    )
    for copy in copies:
        copy.start()
    copies[0].wait()
    out_ref[feat:] = wide[...].astype(jnp.bfloat16)
    copies[1].wait()


def pair_kernel(own_ref, other_ref, pair_ref, points_ref):
    pair_ref[0] = own_ref[...]
    pair_ref[1] = other_ref[...]
    points_ref[...] = own_ref[: points_ref.shape[0]]


def after_kernel(_, *refs):
    for at, ref in enumerate(refs[:-1]):
        refs[-1][at] = ref[...]


def after(before, *blocks):
    return pl.pallas_call(
        after_kernel,
        out_shape=jax.ShapeDtypeStruct((len(blocks), *blocks[0].shape), blocks[0].dtype),
        in_specs=[pl.BlockSpec(memory_space=pl.ANY)]
        + [pl.BlockSpec(memory_space=pltpu.VMEM)] * len(blocks),
        compiler_params=params(),
    )(before, *blocks)


class Row(NamedTuple):
    points: Any
    side: Any = None
    partial: Any = None


class Cols(NamedTuple):
    blocks: Any
    sides: Any = None


def products_kernel(feat, new_rows, begun, new_cols, groups, *refs):
    refs = list(refs)

    def take(count):
        taken = refs[:count]
        del refs[:count]
        return taken

    lengths = take(1)[0][...]
    sources, starts = take(len(new_rows)), take(sum(begun))
    blocks, given = take(len(new_cols)), take(len(new_cols) - sum(new_cols))
    outs, made_rows, made_cols = take(len(new_rows)), take(sum(new_rows)), take(sum(new_cols))
    held = refs[0]
    row_sides, col_sides = [], []
    for is_new, block_ref in zip(new_cols, blocks):
        if not is_new:
            col_sides.append(given.pop(0))
            continue
        col_sides.append(made_cols.pop(0))
        for at in range(block_ref.shape[0]):
            put_col_side(col_sides[-1].at[at], block_ref[at, :feat], lengths)
    for is_new, source in zip(new_rows, sources):
        row_sides.append(made_rows.pop(0) if is_new else source)
        if is_new:
            put_row_side(row_sides[-1], source[:feat], lengths)
    for has_start, out_ref in zip(begun, outs):
        out_ref[...] = starts.pop(0)[...] if has_start else jnp.zeros_like(out_ref)
    add_all(
        [
            (
                [(outs[at], row_sides[at]) for at in rows],
                [(col_sides[at], blocks[at]) for at in cols],
            )
            for rows, cols in groups
        ],
        feat,
        held,
    )


def products(lengths, rhs, rows, cols, groups, weight):
    feat, width = lengths.shape[0], cols[0].blocks.shape[2]
    shape = jax.ShapeDtypeStruct
    new_rows = [row.side is None for row in rows]
    begun = [row.partial is not None for row in rows]
    new_cols = [col.sides is None for col in cols]
    depth = feat + TAIL
    out_shape = (
        [shape((rhs, width), jnp.float32)] * len(rows)
        + [shape((width, depth), jnp.bfloat16)] * sum(new_rows)
        + [
            shape((col.blocks.shape[0], depth, width), jnp.bfloat16)
            for col, is_new in zip(cols, new_cols)
            if is_new
        ]
    )
    made = list(
        pl.pallas_call(
            functools.partial(products_kernel, feat, new_rows, begun, new_cols, groups),
            out_shape=out_shape,
            scratch_shapes=[pltpu.VMEM((width, width), jnp.float32)],
            compiler_params=params(),
            cost_estimate=cost(int(weight * width * width)),
        )(
            lengths,
            *[row.points if row.side is None else row.side for row in rows],
            *[row.partial for row in rows if row.partial is not None],
            *[col.blocks for col in cols],
            *[col.sides for col in cols if col.sides is not None],
        )
    )
    partials = [made.pop(0) for _ in rows]
    sides = [made.pop(0) if is_new else row.side for row, is_new in zip(rows, new_rows)]
    rows = [Row(row.points, side, part) for row, side, part in zip(rows, sides, partials)]
    cols = [Cols(col.blocks, made.pop(0)) if is_new else col for col, is_new in zip(cols, new_cols)]
    return rows, cols


def cost(pairs):
    return pl.CostEstimate(flops=pairs * 768, bytes_accessed=pairs // 4, transcendentals=pairs)


def scattered_kernel(parts, *refs):
    noise_ref, direction_ref, residual_ref = refs[:3]
    image_ref, sums_ref = refs[3 + parts :]
    direction, residual = direction_ref[...], residual_ref[...]
    image = noise_ref[...] * direction
    for ref in refs[3 : 3 + parts]:
        image = image + ref[...]
    image_ref[...] = image
    sums = (
        jnp.sum(residual * residual, axis=1, keepdims=True),
        jnp.sum(direction * image, axis=1, keepdims=True),
        jnp.sum(residual * image, axis=1, keepdims=True),
        jnp.sum(image * image, axis=1, keepdims=True),
    )
    rhs = direction.shape[0]
    lane = lax.broadcasted_iota(jnp.int32, (rhs, 128), 1)
    right = lax.broadcasted_iota(jnp.int32, (rhs, 128), 0)
    packed = jnp.zeros((rhs, 128), jnp.float32)
    for index, value in enumerate(sums):
        packed = jnp.where(lane == index * rhs + right, value, packed)
    row = jnp.sum(packed, axis=0, keepdims=True)
    sums_ref[...] = jnp.broadcast_to(row[None], sums_ref.shape)


def update_kernel(
    solution_ref, residual_ref, direction_ref, image_ref, sums_ref, new_solution, new_residual, new_direction
):
    direction = direction_ref[...]
    rhs = direction.shape[0]
    row = jnp.sum(sums_ref[...], axis=0)
    lane = lax.broadcasted_iota(jnp.int32, (rhs, 128), 1)
    right = lax.broadcasted_iota(jnp.int32, (rhs, 128), 0)
    norm_old, curvature, mixed, image_norm = (
        jnp.sum(jnp.where(lane == index * rhs + right, row, 0.0), axis=1, keepdims=True)
        for index in range(4)
    )
    step = norm_old / curvature
    norm_new = jnp.maximum(norm_old + step * (step * image_norm - 2.0 * mixed), 0.0)
    updated = residual_ref[...] - step * image_ref[...]
    new_solution[...] = solution_ref[...] + step * direction
    new_residual[...] = updated
    new_direction[...] = updated + (norm_new / norm_old) * direction


def swap(array, devices, mask):
    return lax.ppermute(array, AXES, [(at, at ^ mask) for at in range(devices)])


def shift_line(array, devices, steps):
    return lax.ppermute(
        array, AXES, [(at, (at + steps * LINE) % devices) for at in range(devices)]
    )


def local(devices, points, lengths, noise_var, solution, residual, direction):
    f32, bf16 = jnp.float32, jnp.bfloat16
    shape = jax.ShapeDtypeStruct
    feat, width = points.shape
    rhs = direction.shape[0]
    masks = (X + Y, X, Y)
    lengths = lengths[:, None]

    along_x = swap(points, devices, X)
    packed = pl.pallas_call(
        pack_kernel,
        out_shape=shape((feat + rhs, width), bf16),
        in_specs=[pl.BlockSpec(memory_space=pltpu.HBM)] * 2,
        scratch_shapes=[pltpu.VMEM((rhs, width), f32), pltpu.SemaphoreType.DMA((2,))],
        compiler_params=params(),
    )(
        pltpu.with_memory_space_constraint(points, pltpu.HBM),
        pltpu.with_memory_space_constraint(direction, pltpu.HBM),
    )
    pair, near = pl.pallas_call(
        pair_kernel,
        out_shape=[shape((2, feat + rhs, width), bf16), shape((feat, width), bf16)],
        compiler_params=params(),
    )(packed, swap(packed, devices, CORE))
    along_y = swap(near, devices, Y)
    across = swap(along_x, devices, Y)
    add = functools.partial(products, lengths, rhs)

    line = [shift_line(packed, devices, steps) for steps in range(devices // LINE - 1, 0, -1)]
    (own, x_row), (chip,) = add([Row(packed), Row(along_x)], [Cols(pair)], [((0, 1), (0,))], EARLY)
    (x_row, y_row), (_, first) = add(
        [x_row, Row(along_y)], [chip, Cols(line[-1][None])], [((1,), (0,)), ((0, 1), (1,))], EARLY
    )
    (xy_row,), _ = add([Row(across)], [chip, first], [((0,), (0, 1))], EARLY)
    rest = after(xy_row.partial, *line[:-1])
    crossed = swap(after(xy_row.partial, *line), devices, CORE)
    peers, (rest,) = add([xy_row, x_row, y_row], [Cols(rest)], [((0, 1, 2), (0,))], LATE)
    peers, (crossed,) = add(peers, [Cols(crossed)], [((0, 1, 2), (0,))], LATE)
    from_peers = [swap(row.partial, devices, mask) for row, mask in zip(peers, masks)]
    (own,), _ = add([own], [first, rest, crossed], [((0,), (0, 1, 2))], LATE)
    mine = own.partial

    image, sums = pl.pallas_call(
        functools.partial(scattered_kernel, 1 + len(masks)),
        out_shape=[shape((rhs, width), f32), shape((devices, 1, 128), f32)],
        compiler_params=params(),
    )(noise_var[None, :], direction, residual, mine, *from_peers)
    all_sums = lax.all_to_all(sums, AXES, 0, 0, tiled=True)
    return tuple(
        pl.pallas_call(
            update_kernel, out_shape=[shape((rhs, width), f32)] * 3, compiler_params=params()
        )(solution, residual, direction, image, all_sums)
    )


def solution(mesh):
    placed = (
        P(None, AXES),
        P(),
        P(AXES),
        P(None, AXES),
        P(None, AXES),
        P(None, AXES),
    )
    return jax.shard_map(
        functools.partial(local, mesh.shape["row"] * mesh.shape["col"]),
        mesh=mesh,
        in_specs=placed,
        out_specs=(P(None, AXES), P(None, AXES), P(None, AXES)),
        check_vma=False,
    )
```

```python
import functools
from typing import Any, NamedTuple

import jax
import jax.numpy as jnp
from jax import lax
from jax.experimental import pallas as pl
from jax.experimental.pallas import tpu as pltpu
from jax.sharding import PartitionSpec as P

AXES = ("row", "col")
X, Y = 2, 4
CORE = 1
LINE = 8
LOG2E = 1.4426950408889634
TAIL = 16
UNROLL = 16
AHEAD = 2
EARLY, LATE = 0.25, 6
VMEM_LIMIT = 24 * 1024 * 1024


def params():
    return pltpu.CompilerParams(vmem_limit_bytes=VMEM_LIMIT)


def three_pieces(value):
    high = value.astype(jnp.bfloat16).astype(jnp.float32)
    rest = value - high
    middle = rest.astype(jnp.bfloat16).astype(jnp.float32)
    return high, middle, rest - middle


def tail_rows(squares, first):
    count = squares.shape[1]
    high, middle, low = three_pieces(-0.5 * squares)
    at = lax.broadcasted_iota(jnp.int32, (TAIL, count), 0)
    start = 0 if first else 3
    tail = jnp.where(at < 6, 1.0, 0.0)
    tail = jnp.where(at == start, high, tail)
    tail = jnp.where(at == start + 1, middle, tail)
    tail = jnp.where(at == start + 2, low, tail)
    return tail


def scaled_of(points, lengths):
    return (points.astype(jnp.float32) / lengths).astype(jnp.bfloat16)


def squares_of(scaled):
    values = scaled.astype(jnp.float32)
    return jnp.sum(values * values, axis=0, keepdims=True)


def side_of(points, lengths, first):
    scaled = scaled_of(points, lengths)
    tail = tail_rows(squares_of(scaled), first)
    return jnp.concatenate([scaled.astype(jnp.float32), tail], axis=0)


def put_row_side(ref, points, lengths):
    ref[...] = side_of(points, lengths, True).T.astype(jnp.bfloat16)


def put_col_side(ref, points, lengths):
    ref[...] = side_of(points, lengths, False).astype(jnp.bfloat16)


def half_distance(row_ref, col_ref):
    return jnp.dot(row_ref[...], col_ref[...], preferred_element_type=jnp.float32)


def add_product(out_ref, half, weight_ref):
    tile = jnp.exp2(half * LOG2E).astype(jnp.bfloat16)
    out_ref[...] += lax.dot_general(
        weight_ref[...], tile, (((1,), (1,)), ((), ())), preferred_element_type=jnp.float32
    )


def add_all(groups, feat, held):
    def tiles(rows, sides, blocks, begin, count):
        return [
            (out_ref, row_ref, sides.at[begin + at], blocks.at[begin + at, feat:])
            for at in range(count)
            for out_ref, row_ref in rows
        ]

    def run(order, half, last):
        halves, made = [half], 1
        for place, (out_ref, _, _, weight_ref) in enumerate(order):
            while made < min(place + 1 + AHEAD, len(order)):
                halves.append(half_distance(*order[made][1:3]))
                made += 1
            if place + 1 == len(order):
                last()
            add_product(out_ref, halves.pop(0), weight_ref)

    pieces = [(rows, sides, blocks) for rows, cols in groups for sides, blocks in cols]
    if sum(len(rows) * sides.shape[0] for rows, sides, _ in pieces) <= UNROLL:
        order = [tile for piece in pieces for tile in tiles(*piece, 0, piece[1].shape[0])]
        run(order, half_distance(*order[0][1:3]), lambda: None)
        return

    for rows, sides, blocks in pieces:
        cols = sides.shape[0]
        group = max(
            at for at in range(1, cols + 1) if cols % at == 0 and (at == 1 or at * len(rows) <= UNROLL)
        )

        def following(begin):
            held[...] = half_distance(rows[0][1], sides.at[begin])

        def body(index, _):
            order = tiles(rows, sides, blocks, index * group, group)
            run(order, held[...], lambda: following((index + 1) * group))
            return 0

        following(0)
        steps = cols // group
        lax.fori_loop(0, steps - 1, body, 0)
        run(tiles(rows, sides, blocks, (steps - 1) * group, group), held[...], lambda: None)


def pack_kernel(points_ref, direction_ref, out_ref, wide, sems):
    feat = points_ref.shape[0]
    copies = (
        pltpu.make_async_copy(direction_ref, wide, sems.at[0]),
        pltpu.make_async_copy(points_ref, out_ref.at[:feat], sems.at[1]),
    )
    for copy in copies:
        copy.start()
    copies[0].wait()
    out_ref[feat:] = wide[...].astype(jnp.bfloat16)
    copies[1].wait()


def pair_kernel(own_ref, other_ref, pair_ref, points_ref):
    pair_ref[0] = own_ref[...]
    pair_ref[1] = other_ref[...]
    points_ref[...] = own_ref[: points_ref.shape[0]]


def after_kernel(_, *refs):
    for at, ref in enumerate(refs[:-1]):
        refs[-1][at] = ref[...]


def after(before, *blocks):
    return pl.pallas_call(
        after_kernel,
        out_shape=jax.ShapeDtypeStruct((len(blocks), *blocks[0].shape), blocks[0].dtype),
        in_specs=[pl.BlockSpec(memory_space=pl.ANY)]
        + [pl.BlockSpec(memory_space=pltpu.VMEM)] * len(blocks),
        compiler_params=params(),
    )(before, *blocks)


class Row(NamedTuple):
    points: Any
    side: Any = None
    partial: Any = None


class Cols(NamedTuple):
    blocks: Any
    sides: Any = None


def products_kernel(feat, new_rows, begun, new_cols, groups, *refs):
    refs = list(refs)

    def take(count):
        taken = refs[:count]
        del refs[:count]
        return taken

    lengths = take(1)[0][...]
    sources, starts = take(len(new_rows)), take(sum(begun))
    blocks, given = take(len(new_cols)), take(len(new_cols) - sum(new_cols))
    outs, made_rows, made_cols = take(len(new_rows)), take(sum(new_rows)), take(sum(new_cols))
    held = refs[0]
    row_sides, col_sides = [], []
    for is_new, block_ref in zip(new_cols, blocks):
        if not is_new:
            col_sides.append(given.pop(0))
            continue
        col_sides.append(made_cols.pop(0))
        for at in range(block_ref.shape[0]):
            put_col_side(col_sides[-1].at[at], block_ref[at, :feat], lengths)
    for is_new, source in zip(new_rows, sources):
        row_sides.append(made_rows.pop(0) if is_new else source)
        if is_new:
            put_row_side(row_sides[-1], source[:feat], lengths)
    for has_start, out_ref in zip(begun, outs):
        out_ref[...] = starts.pop(0)[...] if has_start else jnp.zeros_like(out_ref)
    add_all(
        [
            (
                [(outs[at], row_sides[at]) for at in rows],
                [(col_sides[at], blocks[at]) for at in cols],
            )
            for rows, cols in groups
        ],
        feat,
        held,
    )


def products(lengths, rhs, rows, cols, groups, weight):
    feat, width = lengths.shape[0], cols[0].blocks.shape[2]
    shape = jax.ShapeDtypeStruct
    new_rows = [row.side is None for row in rows]
    begun = [row.partial is not None for row in rows]
    new_cols = [col.sides is None for col in cols]
    depth = feat + TAIL
    out_shape = (
        [shape((rhs, width), jnp.float32)] * len(rows)
        + [shape((width, depth), jnp.bfloat16)] * sum(new_rows)
        + [
            shape((col.blocks.shape[0], depth, width), jnp.bfloat16)
            for col, is_new in zip(cols, new_cols)
            if is_new
        ]
    )
    made = list(
        pl.pallas_call(
            functools.partial(products_kernel, feat, new_rows, begun, new_cols, groups),
            out_shape=out_shape,
            scratch_shapes=[pltpu.VMEM((width, width), jnp.float32)],
            compiler_params=params(),
            cost_estimate=cost(int(weight * width * width)),
        )(
            lengths,
            *[row.points if row.side is None else row.side for row in rows],
            *[row.partial for row in rows if row.partial is not None],
            *[col.blocks for col in cols],
            *[col.sides for col in cols if col.sides is not None],
        )
    )
    partials = [made.pop(0) for _ in rows]
    sides = [made.pop(0) if is_new else row.side for row, is_new in zip(rows, new_rows)]
    rows = [Row(row.points, side, part) for row, side, part in zip(rows, sides, partials)]
    cols = [Cols(col.blocks, made.pop(0)) if is_new else col for col, is_new in zip(cols, new_cols)]
    return rows, cols


def cost(pairs):
    return pl.CostEstimate(flops=pairs * 768, bytes_accessed=pairs // 4, transcendentals=pairs)


def scattered_kernel(parts, *refs):
    noise_ref, direction_ref, residual_ref = refs[:3]
    image_ref, sums_ref = refs[3 + parts :]
    direction, residual = direction_ref[...], residual_ref[...]
    image = noise_ref[...] * direction
    for ref in refs[3 : 3 + parts]:
        image = image + ref[...]
    image_ref[...] = image
    sums = (
        jnp.sum(residual * residual, axis=1, keepdims=True),
        jnp.sum(direction * image, axis=1, keepdims=True),
        jnp.sum(residual * image, axis=1, keepdims=True),
        jnp.sum(image * image, axis=1, keepdims=True),
    )
    rhs = direction.shape[0]
    lane = lax.broadcasted_iota(jnp.int32, (rhs, 128), 1)
    right = lax.broadcasted_iota(jnp.int32, (rhs, 128), 0)
    packed = jnp.zeros((rhs, 128), jnp.float32)
    for index, value in enumerate(sums):
        packed = jnp.where(lane == index * rhs + right, value, packed)
    row = jnp.sum(packed, axis=0, keepdims=True)
    sums_ref[...] = jnp.broadcast_to(row[None], sums_ref.shape)


def update_kernel(
    solution_ref, residual_ref, direction_ref, image_ref, sums_ref, new_solution, new_residual, new_direction
):
    direction = direction_ref[...]
    rhs = direction.shape[0]
    row = jnp.sum(sums_ref[...], axis=0)
    lane = lax.broadcasted_iota(jnp.int32, (rhs, 128), 1)
    right = lax.broadcasted_iota(jnp.int32, (rhs, 128), 0)
    norm_old, curvature, mixed, image_norm = (
        jnp.sum(jnp.where(lane == index * rhs + right, row, 0.0), axis=1, keepdims=True)
        for index in range(4)
    )
    step = norm_old / curvature
    norm_new = jnp.maximum(norm_old + step * (step * image_norm - 2.0 * mixed), 0.0)
    updated = residual_ref[...] - step * image_ref[...]
    new_solution[...] = solution_ref[...] + step * direction
    new_residual[...] = updated
    new_direction[...] = updated + (norm_new / norm_old) * direction


def swap(array, devices, mask):
    return lax.ppermute(array, AXES, [(at, at ^ mask) for at in range(devices)])


def shift_line(array, devices, steps):
    return lax.ppermute(
        array, AXES, [(at, (at + steps * LINE) % devices) for at in range(devices)]
    )


def local(devices, points, lengths, noise_var, solution, residual, direction):
    f32, bf16 = jnp.float32, jnp.bfloat16
    shape = jax.ShapeDtypeStruct
    feat, width = points.shape
    rhs = direction.shape[0]
    masks = (X + Y, X, Y)
    lengths = lengths[:, None]

    along_x = swap(points, devices, X)
    packed = pl.pallas_call(
        pack_kernel,
        out_shape=shape((feat + rhs, width), bf16),
        in_specs=[pl.BlockSpec(memory_space=pltpu.HBM)] * 2,
        scratch_shapes=[pltpu.VMEM((rhs, width), f32), pltpu.SemaphoreType.DMA((2,))],
        compiler_params=params(),
    )(
        pltpu.with_memory_space_constraint(points, pltpu.HBM),
        pltpu.with_memory_space_constraint(direction, pltpu.HBM),
    )
    pair, near = pl.pallas_call(
        pair_kernel,
        out_shape=[shape((2, feat + rhs, width), bf16), shape((feat, width), bf16)],
        compiler_params=params(),
    )(packed, swap(packed, devices, CORE))
    along_y = swap(near, devices, Y)
    across = swap(along_x, devices, Y)
    add = functools.partial(products, lengths, rhs)

    line = [shift_line(packed, devices, steps) for steps in range(devices // LINE - 1, 0, -1)]
    (own, x_row), (chip,) = add([Row(packed), Row(along_x)], [Cols(pair)], [((0, 1), (0,))], EARLY)
    (x_row, y_row), (_, first) = add(
        [x_row, Row(along_y)], [chip, Cols(line[-1][None])], [((1,), (0,)), ((0, 1), (1,))], EARLY
    )
    (xy_row,), _ = add([Row(across)], [chip, first], [((0,), (0, 1))], EARLY)
    rest = after(xy_row.partial, *line[:-1])
    crossed = swap(after(xy_row.partial, *line), devices, CORE)
    peers, (rest,) = add([xy_row, x_row, y_row], [Cols(rest)], [((0, 1, 2), (0,))], LATE)
    peers, (crossed,) = add(peers, [Cols(crossed)], [((0, 1, 2), (0,))], LATE)
    from_peers = [swap(row.partial, devices, mask) for row, mask in zip(peers, masks)]
    (own,), _ = add([own], [first, rest, crossed], [((0,), (0, 1, 2))], LATE)
    mine = own.partial

    image, sums = pl.pallas_call(
        functools.partial(scattered_kernel, 1 + len(masks)),
        out_shape=[shape((rhs, width), f32), shape((devices, 1, 128), f32)],
        compiler_params=params(),
    )(noise_var[None, :], direction, residual, mine, *from_peers)
    all_sums = lax.all_to_all(sums, AXES, 0, 0, tiled=True)
    return tuple(
        pl.pallas_call(
            update_kernel, out_shape=[shape((rhs, width), f32)] * 3, compiler_params=params()
        )(solution, residual, direction, image, all_sums)
    )


def solution(mesh):
    placed = (
        P(None, AXES),
        P(),
        P(AXES),
        P(None, AXES),
        P(None, AXES),
        P(None, AXES),
    )
    return jax.shard_map(
        functools.partial(local, mesh.shape["row"] * mesh.shape["col"]),
        mesh=mesh,
        in_specs=placed,
        out_specs=(P(None, AXES), P(None, AXES), P(None, AXES)),
        check_vma=False,
    )
```

```python
import functools
from typing import Any, NamedTuple

import jax
import jax.numpy as jnp
from jax import lax
from jax.experimental import pallas as pl
from jax.experimental.pallas import tpu as pltpu
from jax.sharding import PartitionSpec as P

AXES = ("row", "col")
X, Y = 2, 4
CORE = 1
LINE = 8
LOG2E = 1.4426950408889634
TAIL = 16
UNROLL = 16
EARLY, LATE = 0.25, 6
VMEM_LIMIT = 24 * 1024 * 1024


def params():
    return pltpu.CompilerParams(vmem_limit_bytes=VMEM_LIMIT)


def three_pieces(value):
    high = value.astype(jnp.bfloat16).astype(jnp.float32)
    rest = value - high
    middle = rest.astype(jnp.bfloat16).astype(jnp.float32)
    return high, middle, rest - middle


def tail_rows(squares, first):
    count = squares.shape[1]
    high, middle, low = three_pieces(-0.5 * squares)
    at = lax.broadcasted_iota(jnp.int32, (TAIL, count), 0)
    start = 0 if first else 3
    tail = jnp.where(at < 6, 1.0, 0.0)
    tail = jnp.where(at == start, high, tail)
    tail = jnp.where(at == start + 1, middle, tail)
    tail = jnp.where(at == start + 2, low, tail)
    return tail


def scaled_of(points, lengths):
    return (points.astype(jnp.float32) / lengths).astype(jnp.bfloat16)


def squares_of(scaled):
    values = scaled.astype(jnp.float32)
    return jnp.sum(values * values, axis=0, keepdims=True)


def side_of(points, lengths, first):
    scaled = scaled_of(points, lengths)
    tail = tail_rows(squares_of(scaled), first)
    return jnp.concatenate([scaled.astype(jnp.float32), tail], axis=0)


def put_row_side(ref, points, lengths):
    ref[...] = side_of(points, lengths, True).T.astype(jnp.bfloat16)


def put_col_side(ref, points, lengths):
    ref[...] = side_of(points, lengths, False).astype(jnp.bfloat16)


def half_distance(row_ref, col_ref):
    return jnp.dot(row_ref[...], col_ref[...], preferred_element_type=jnp.float32)


def add_product(out_ref, half, weight_ref):
    tile = jnp.exp2(half * LOG2E).astype(jnp.bfloat16)
    out_ref[...] += lax.dot_general(
        weight_ref[...], tile, (((1,), (1,)), ((), ())), preferred_element_type=jnp.float32
    )


def add_all(groups, feat, held):
    def tiles(rows, sides, blocks, begin, count):
        return [
            (out_ref, row_ref, sides.at[begin + at], blocks.at[begin + at, feat:])
            for at in range(count)
            for out_ref, row_ref in rows
        ]

    def run(order, half, last):
        for place, (out_ref, _, _, weight_ref) in enumerate(order):
            if place + 1 < len(order):
                ahead = half_distance(*order[place + 1][1:3])
            else:
                ahead = last()
            add_product(out_ref, half, weight_ref)
            half = ahead

    pieces = [(rows, sides, blocks) for rows, cols in groups for sides, blocks in cols]
    if sum(len(rows) * sides.shape[0] for rows, sides, _ in pieces) <= UNROLL:
        order = [tile for piece in pieces for tile in tiles(*piece, 0, piece[1].shape[0])]
        run(order, half_distance(*order[0][1:3]), lambda: None)
        return

    for rows, sides, blocks in pieces:
        cols = sides.shape[0]
        group = max(
            at for at in range(1, cols + 1) if cols % at == 0 and (at == 1 or at * len(rows) <= UNROLL)
        )

        def following(begin):
            held[...] = half_distance(rows[0][1], sides.at[begin])

        def body(index, _):
            order = tiles(rows, sides, blocks, index * group, group)
            run(order, held[...], lambda: following((index + 1) * group))
            return 0

        following(0)
        steps = cols // group
        lax.fori_loop(0, steps - 1, body, 0)
        run(tiles(rows, sides, blocks, (steps - 1) * group, group), held[...], lambda: None)


def pack_kernel(points_ref, direction_ref, out_ref, wide, sems):
    feat = points_ref.shape[0]
    copies = (
        pltpu.make_async_copy(direction_ref, wide, sems.at[0]),
        pltpu.make_async_copy(points_ref, out_ref.at[:feat], sems.at[1]),
    )
    for copy in copies:
        copy.start()
    copies[0].wait()
    out_ref[feat:] = wide[...].astype(jnp.bfloat16)
    copies[1].wait()


def pair_kernel(own_ref, other_ref, pair_ref, points_ref):
    pair_ref[0] = own_ref[...]
    pair_ref[1] = other_ref[...]
    points_ref[...] = own_ref[: points_ref.shape[0]]


def after_kernel(_, *refs):
    for at, ref in enumerate(refs[:-1]):
        refs[-1][at] = ref[...]


def after(before, *blocks):
    return pl.pallas_call(
        after_kernel,
        out_shape=jax.ShapeDtypeStruct((len(blocks), *blocks[0].shape), blocks[0].dtype),
        in_specs=[pl.BlockSpec(memory_space=pl.ANY)]
        + [pl.BlockSpec(memory_space=pltpu.VMEM)] * len(blocks),
        compiler_params=params(),
    )(before, *blocks)


class Row(NamedTuple):
    points: Any
    side: Any = None
    partial: Any = None


class Cols(NamedTuple):
    blocks: Any
    sides: Any = None


def products_kernel(feat, new_rows, begun, new_cols, groups, *refs):
    refs = list(refs)

    def take(count):
        taken = refs[:count]
        del refs[:count]
        return taken

    lengths = take(1)[0][...]
    sources, starts = take(len(new_rows)), take(sum(begun))
    blocks, given = take(len(new_cols)), take(len(new_cols) - sum(new_cols))
    outs, made_rows, made_cols = take(len(new_rows)), take(sum(new_rows)), take(sum(new_cols))
    held = refs[0]
    row_sides, col_sides = [], []
    for is_new, block_ref in zip(new_cols, blocks):
        if not is_new:
            col_sides.append(given.pop(0))
            continue
        col_sides.append(made_cols.pop(0))
        for at in range(block_ref.shape[0]):
            put_col_side(col_sides[-1].at[at], block_ref[at, :feat], lengths)
    for is_new, source in zip(new_rows, sources):
        row_sides.append(made_rows.pop(0) if is_new else source)
        if is_new:
            put_row_side(row_sides[-1], source[:feat], lengths)
    for has_start, out_ref in zip(begun, outs):
        out_ref[...] = starts.pop(0)[...] if has_start else jnp.zeros_like(out_ref)
    add_all(
        [
            (
                [(outs[at], row_sides[at]) for at in rows],
                [(col_sides[at], blocks[at]) for at in cols],
            )
            for rows, cols in groups
        ],
        feat,
        held,
    )


def products(lengths, rhs, rows, cols, groups, weight):
    feat, width = lengths.shape[0], cols[0].blocks.shape[2]
    shape = jax.ShapeDtypeStruct
    new_rows = [row.side is None for row in rows]
    begun = [row.partial is not None for row in rows]
    new_cols = [col.sides is None for col in cols]
    depth = feat + TAIL
    out_shape = (
        [shape((rhs, width), jnp.float32)] * len(rows)
        + [shape((width, depth), jnp.bfloat16)] * sum(new_rows)
        + [
            shape((col.blocks.shape[0], depth, width), jnp.bfloat16)
            for col, is_new in zip(cols, new_cols)
            if is_new
        ]
    )
    made = list(
        pl.pallas_call(
            functools.partial(products_kernel, feat, new_rows, begun, new_cols, groups),
            out_shape=out_shape,
            scratch_shapes=[pltpu.VMEM((width, width), jnp.float32)],
            compiler_params=params(),
            cost_estimate=cost(int(weight * width * width)),
        )(
            lengths,
            *[row.points if row.side is None else row.side for row in rows],
            *[row.partial for row in rows if row.partial is not None],
            *[col.blocks for col in cols],
            *[col.sides for col in cols if col.sides is not None],
        )
    )
    partials = [made.pop(0) for _ in rows]
    sides = [made.pop(0) if is_new else row.side for row, is_new in zip(rows, new_rows)]
    rows = [Row(row.points, side, part) for row, side, part in zip(rows, sides, partials)]
    cols = [Cols(col.blocks, made.pop(0)) if is_new else col for col, is_new in zip(cols, new_cols)]
    return rows, cols


def cost(pairs):
    return pl.CostEstimate(flops=pairs * 768, bytes_accessed=pairs // 4, transcendentals=pairs)


def scattered_kernel(parts, *refs):
    noise_ref, direction_ref, residual_ref = refs[:3]
    image_ref, sums_ref = refs[3 + parts :]
    direction, residual = direction_ref[...], residual_ref[...]
    image = noise_ref[...] * direction
    for ref in refs[3 : 3 + parts]:
        image = image + ref[...]
    image_ref[...] = image
    sums = (
        jnp.sum(residual * residual, axis=1, keepdims=True),
        jnp.sum(direction * image, axis=1, keepdims=True),
        jnp.sum(residual * image, axis=1, keepdims=True),
        jnp.sum(image * image, axis=1, keepdims=True),
    )
    rhs = direction.shape[0]
    lane = lax.broadcasted_iota(jnp.int32, (rhs, 128), 1)
    right = lax.broadcasted_iota(jnp.int32, (rhs, 128), 0)
    packed = jnp.zeros((rhs, 128), jnp.float32)
    for index, value in enumerate(sums):
        packed = jnp.where(lane == index * rhs + right, value, packed)
    row = jnp.sum(packed, axis=0, keepdims=True)
    sums_ref[...] = jnp.broadcast_to(row[None], sums_ref.shape)


def update_kernel(
    solution_ref, residual_ref, direction_ref, image_ref, sums_ref, new_solution, new_residual, new_direction
):
    direction = direction_ref[...]
    rhs = direction.shape[0]
    row = jnp.sum(sums_ref[...], axis=0)
    lane = lax.broadcasted_iota(jnp.int32, (rhs, 128), 1)
    right = lax.broadcasted_iota(jnp.int32, (rhs, 128), 0)
    norm_old, curvature, mixed, image_norm = (
        jnp.sum(jnp.where(lane == index * rhs + right, row, 0.0), axis=1, keepdims=True)
        for index in range(4)
    )
    step = norm_old / curvature
    norm_new = jnp.maximum(norm_old + step * (step * image_norm - 2.0 * mixed), 0.0)
    updated = residual_ref[...] - step * image_ref[...]
    new_solution[...] = solution_ref[...] + step * direction
    new_residual[...] = updated
    new_direction[...] = updated + (norm_new / norm_old) * direction


def swap(array, devices, mask):
    return lax.ppermute(array, AXES, [(at, at ^ mask) for at in range(devices)])


def shift_line(array, devices, steps):
    return lax.ppermute(
        array, AXES, [(at, (at + steps * LINE) % devices) for at in range(devices)]
    )


def local(devices, points, lengths, noise_var, solution, residual, direction):
    f32, bf16 = jnp.float32, jnp.bfloat16
    shape = jax.ShapeDtypeStruct
    feat, width = points.shape
    rhs = direction.shape[0]
    masks = (X + Y, X, Y)
    lengths = lengths[:, None]

    along_x = swap(points, devices, X)
    packed = pl.pallas_call(
        pack_kernel,
        out_shape=shape((feat + rhs, width), bf16),
        in_specs=[pl.BlockSpec(memory_space=pltpu.HBM)] * 2,
        scratch_shapes=[pltpu.VMEM((rhs, width), f32), pltpu.SemaphoreType.DMA((2,))],
        compiler_params=params(),
    )(
        pltpu.with_memory_space_constraint(points, pltpu.HBM),
        pltpu.with_memory_space_constraint(direction, pltpu.HBM),
    )
    pair, near = pl.pallas_call(
        pair_kernel,
        out_shape=[shape((2, feat + rhs, width), bf16), shape((feat, width), bf16)],
        compiler_params=params(),
    )(packed, swap(packed, devices, CORE))
    along_y = swap(near, devices, Y)
    across = swap(along_x, devices, Y)
    add = functools.partial(products, lengths, rhs)

    line = [shift_line(packed, devices, steps) for steps in range(devices // LINE - 1, 0, -1)]
    (x_row,), (chip,) = add([Row(along_x)], [Cols(pair)], [((0,), (0,))], EARLY)
    (x_row, y_row), (_, first) = add(
        [x_row, Row(along_y)], [chip, Cols(line[-1][None])], [((1,), (0,)), ((0, 1), (1,))], EARLY
    )
    (xy_row,), _ = add([Row(across)], [chip, first], [((0,), (0, 1))], EARLY)
    rest = after(xy_row.partial, *line[:-1])
    crossed = swap(after(xy_row.partial, *line), devices, CORE)
    peers, (rest,) = add([xy_row, x_row, y_row], [Cols(rest)], [((0, 1, 2), (0,))], LATE)
    peers, (crossed,) = add(peers, [Cols(crossed)], [((0, 1, 2), (0,))], LATE)
    from_peers = [swap(row.partial, devices, mask) for row, mask in zip(peers, masks)]
    (own,), _ = add([Row(packed)], [chip, first, rest, crossed], [((0,), (0, 1, 2, 3))], LATE)
    mine = own.partial

    image, sums = pl.pallas_call(
        functools.partial(scattered_kernel, 1 + len(masks)),
        out_shape=[shape((rhs, width), f32), shape((devices, 1, 128), f32)],
        compiler_params=params(),
    )(noise_var[None, :], direction, residual, mine, *from_peers)
    all_sums = lax.all_to_all(sums, AXES, 0, 0, tiled=True)
    return tuple(
        pl.pallas_call(
            update_kernel, out_shape=[shape((rhs, width), f32)] * 3, compiler_params=params()
        )(solution, residual, direction, image, all_sums)
    )


def solution(mesh):
    placed = (
        P(None, AXES),
        P(),
        P(AXES),
        P(None, AXES),
        P(None, AXES),
        P(None, AXES),
    )
    return jax.shard_map(
        functools.partial(local, mesh.shape["row"] * mesh.shape["col"]),
        mesh=mesh,
        in_specs=placed,
        out_specs=(P(None, AXES), P(None, AXES), P(None, AXES)),
        check_vma=False,
    )
```
